256 devices in a mesh: prow: 16 (over x_lo, z), pcol: 16 (over x_hi, y, core).
Axes of the slice: x: 4 (x_hi: 2, x_lo: 2; x = x_hi * 2 + x_lo), y: 4, z: 8, core: 2. Of those that a mesh axis runs over, the one named last changes fastest.
Arguments:
- inverse_blocks: bfloat16 [3, 2, 16, 512, 2, 16, 512], P(None, None, 'prow', None, None, 'pcol'), may hold values from -0.375 to 0.375
- factor_cols: bfloat16 [3, 2, 16, 512, 512], P(None, None, 'prow', 'pcol'), may hold values from -0.23925781 to 0.23925781
- diag_inverse: float32 [3, 512, 512], replicated, may hold values from -6 to 6
- block_mask: int32 [3, 32, 32], replicated, may hold values 0 or 1
Outputs:
- inverse_cols: float32 [3, 2, 16, 512, 512], P(None, None, 'prow', 'pcol')
- inverse_diag: float32 [3, 512, 512], replicated
The draws below stay inside these ranges and needn't reach their ends.
All inputs are finite; a program needn't handle non-finite values.
Results may differ from the reference program's by a relative error of at most 0.0003.
Values may be sent and summed in bfloat16 or wider, within the bound.
A program may use at most 128 MiB of HBM per device.

```python
import jax
import jax.numpy as jnp
from jax import lax

B = 512
NB = 32
NSUP = 3
S = 16384
N_PROW = 16
N_PCOL = 16


def plant(entries, key, smallest, high):
    longest = entries.shape.index(max(entries.shape))
    spots = []
    for shift in (0, 1):
        where = [jax.random.randint(jax.random.fold_in(key, axis), (), 0, length) for axis, length in enumerate(entries.shape)]
        where[longest] = (where[longest] + shift) % entries.shape[longest]
        spots.append(tuple(where))
    return entries.at[spots[0]].set(smallest).at[spots[1]].set(high)


def block_scale(rng, dims, pieces, low, largest):
    loudness = 1.0
    for position, parts in pieces:
        heights = jax.random.uniform(jax.random.fold_in(jax.random.fold_in(rng, 6), position), (parts,), jnp.float32, low / len(pieces), largest / len(pieces))
        loudness = loudness * jnp.repeat(jnp.exp(heights), dims[position] // parts).reshape((-1,) + (1,) * (len(dims) - 1 - position))
    return loudness


def normal_values(key, shape, scale, reach, cuts=(), kind=jnp.bfloat16):
    drawn = scale * jax.random.normal(key, shape, jnp.float32)
    if cuts:
        drawn = drawn * block_scale(key, shape, cuts, -0.22, 0.18)
    return jnp.clip(drawn, -reach, reach).astype(kind)


def setup_inputs(seed: int = 0) -> dict:
    key_list = jax.random.split(jax.random.key(seed), 5)
    return {
        "inverse_blocks": normal_values(key_list[0], (NSUP, NB // N_PROW, N_PROW, B, NB // N_PCOL, N_PCOL, B), (S // 64) ** -0.5, 0.375, ((2, 16), (5, 16))),
        "factor_cols": normal_values(key_list[1], (NSUP, NB // N_PROW, N_PROW, B, B), 0.04, 0.23925781, ((2, 16), (3, 16))),
        "diag_inverse": normal_values(key_list[2], (NSUP, B, B), 1.0, 6.0, (), jnp.float32),
        "block_mask": plant((jax.random.randint(key_list[3], (NSUP, NB, NB), 0, 4) < 3).astype(jnp.int32), jax.random.fold_in(key_list[3], 1), 0, 1),
    }


def reference(inverse_blocks, factor_cols, diag_inverse, block_mask):
    size = NB * B
    full = inverse_blocks.reshape(NSUP, NB, B, size)
    factor = factor_cols.reshape(NSUP, size, B).astype(jnp.float32)

    def per_node(node):
        rows_all = full[node]
        factor_node = factor[node]
        mask_node = block_mask[node].astype(jnp.float32)

        def per_block(index):
            block_row = rows_all[index].astype(jnp.float32)
            scale = jnp.repeat(mask_node[index], B)
            return -jnp.dot(block_row * scale[None, :], factor_node, precision=lax.Precision.HIGHEST)

        columns = lax.map(per_block, jnp.arange(NB, dtype=jnp.int32)).reshape(size, B)
        diagonal = diag_inverse[node] - jnp.dot(factor_node.T, columns, precision=lax.Precision.HIGHEST)
        return columns, diagonal

    columns, diagonal = lax.map(per_node, jnp.arange(NSUP, dtype=jnp.int32))
    return columns.reshape(NSUP, NB // N_PROW, N_PROW, B, B), diagonal
```

```python
import jax
import jax.numpy as jnp
from jax import lax
from jax.experimental import pallas as pl
from jax.experimental.pallas import tpu as pltpu
from jax.sharding import PartitionSpec as P

MESH = pl.DeviceIdType.MESH
F32 = jnp.float32
BF16 = jnp.bfloat16
I32 = jnp.int32

NODES = 3
ZS = 8
YS = 4
CHIPS = 8
ROWS = 16
PIECE = 32
T_WORDS = 136
G_WORDS = 72


def scale_of(code):
    value = code.astype(F32)
    return jnp.where(code > 0, value * (2.0**-8), value * (-(2.0**-30)))


def pack_into(ref, x):
    rows = x.shape[0]
    top = jnp.max(jnp.max(jnp.abs(x), axis=0, keepdims=True), axis=1, keepdims=True)
    coarse = jnp.ceil(top * 256.0).astype(I32)
    fine = -jnp.maximum(jnp.ceil(jnp.minimum(top, 1.0) * (2.0**30)), 1.0).astype(I32)
    code = jnp.where(top >= 1.0, coarse, fine)
    inverse = 32767.0 / scale_of(code)
    q = jnp.floor(x * inverse + 0.5).astype(I32)
    for half in range(2):
        upper = q[:, half * 128 : half * 128 + 128]
        lower = q[:, 256 + half * 128 : 384 + half * 128]
        ref[half * rows : half * rows + rows, :] = (upper << 16) | (lower & 0xFFFF)
    ref[2 * rows : 2 * rows + 8, :] = jnp.broadcast_to(code, (8, 128))


def unpack(ref, rows):
    step = scale_of(ref[2 * rows : 2 * rows + 8, :])[0:1, :] * (1.0 / 32767.0)
    parts = []
    words = [ref[half * rows : half * rows + rows, :] for half in range(2)]
    for word in words:
        parts.append((word >> 16).astype(F32) * step)
    for word in words:
        parts.append(((word << 16) >> 16).astype(F32) * step)
    return jnp.concatenate(parts, axis=1)


def kernel(
    blocks, factor_in, mask, cols_out, diag_out,
    raw, dense, factor, middle, gathered, row_factor, term, split, other, send_t, recv_t, cols,
    own_g, other_g, send_g, recv_g, tiles, recv_tiles, final, packed, diag,
    a_sem, l_sem, p_sem, q_sem, r_sem, m_sem, ring_send, ring_recv, core_send, core_recv,
    t_sem, c_sem, d_sem, g_sem, u_sem, f_sem, h_sem, k_sem, o_sem,
):
    r = lax.axis_index("prow")
    c = lax.axis_index("pcol")
    x_lo, z = r // ZS, r % ZS
    x_hi, y, core = c // (2 * YS), (c // 2) % YS, c % 2
    chip = c // 2
    mate = (r, chip * 2 + (1 - core))
    shift = y + YS * core
    origin = (z + ZS - shift) % ZS
    target = x_lo * ZS + origin

    def slot_at(where):
        gap = (where + ZS - c % ZS) % ZS
        return (gap % YS) * 2 + gap // YS

    def row_peer(d):
        return ((x_lo + d // ZS) % 2) * ZS + (z + d % ZS) % ZS

    def chip_peer(d):
        return ((x_hi + d // YS) % 2) * YS + (y + d % YS) % YS

    def remote(src, dst, send, recv, where):
        return pltpu.make_async_remote_copy(
            src_ref=src, dst_ref=dst, send_sem=send, recv_sem=recv, device_id=where, device_id_type=MESH
        )

    def landed(ref, sem):
        pltpu.make_async_copy(ref, ref, sem).wait()

    own_load = pltpu.make_async_copy(factor_in, factor, l_sem.at[0])
    own_load.start()
    loads = [
        pltpu.make_async_copy(blocks.at[s], raw.at[s], a_sem.at[s]) for s in range(NODES)
    ]
    for load in loads:
        load.start()

    barrier = pltpu.get_barrier_semaphore()

    def greet(where):
        pl.semaphore_signal(barrier, inc=1, device_id=where, device_id_type=MESH)

    same_lo = (r, target)
    other_lo = ((r + ZS) % ROWS, target)
    sources = [((c // ZS) * ZS + z, half * ZS + slot_at(z)) for half in range(2)]

    @pl.when(c != target)
    def _():
        greet(same_lo)

    greet(other_lo)
    for source in sources:
        mine = jnp.logical_and(source[0] == r, source[1] == c)

        @pl.when(jnp.logical_not(mine))
        def _():
            greet(source)

    greet(mate)

    def greet_row(d, carry):
        greet((row_peer(d), c))
        return carry

    lax.fori_loop(1, ROWS, greet_row, 0)

    def greet_chip(d, carry):
        greet((r, chip_peer(d) * 2 + core))
        return carry

    lax.fori_loop(1, CHIPS, greet_chip, 0)
    own_load.wait()

    @pl.when(c != target)
    def _():
        pl.semaphore_wait(barrier, 4 + 1 + (ROWS - 1) + (CHIPS - 1))

    @pl.when(c == target)
    def _():
        pl.semaphore_wait(barrier, 2 + 1 + (ROWS - 1) + (CHIPS - 1))

    def first_hop(s):
        where = (x_lo * ZS + (z + shift) % ZS, c)
        return remote(factor.at[s], middle.at[s], p_sem.at[s, 0], p_sem.at[s, 1], where)

    for s in range(NODES):

        @pl.when(shift != 0)
        def _():
            first_hop(s).start()

        @pl.when(shift == 0)
        def _():
            pltpu.make_async_copy(factor.at[s], middle.at[s], p_sem.at[s, 1]).start()

    def second_hop(s, way):
        where = same_lo if way == 0 else other_lo
        return remote(
            middle.at[s], gathered.at[s, :, c // ZS, c % ZS], q_sem.at[s, way], r_sem.at[s], where
        )

    def forward_piece(s):
        landed(middle.at[s], p_sem.at[s, 1])
        second_hop(s, 1).start()

        @pl.when(c != target)
        def _():
            second_hop(s, 0).start()

        @pl.when(c == target)
        def _():
            pltpu.make_async_copy(middle.at[s], gathered.at[s, :, c // ZS, c % ZS], r_sem.at[s]).start()

    def row_copy(s, d):
        return remote(
            factor.at[s], row_factor.at[s, :, chip, core], m_sem.at[s, 0], m_sem.at[s, 1],
            (r, chip_peer(d) * 2 + core),
        )

    def spread_rows(s):
        def body(d, carry):
            row_copy(s, d).start()
            return carry

        lax.fori_loop(1, CHIPS, body, 0)
        row_factor[s, :, chip, core] = factor[s]

    def rows_copy(s):
        ref = row_factor.at[s, :, :, core]
        return remote(ref, ref, m_sem.at[s, 2], m_sem.at[s, 3], mate)

    def share_rows(s):
        landed(row_factor.at[s, :, pl.ds(0, CHIPS - 1), core], m_sem.at[s, 1])
        rows_copy(s).start()

    right = (x_lo * ZS + (z + 1) % ZS, c)
    left = (x_lo * ZS + (z + ZS - 1) % ZS, c)

    def ring_copy(s, q, k, way):
        if way == 0:
            shard, where = slot_at((z + ZS - (k - 1)) % ZS), right
        else:
            shard, where = slot_at((z + (k - 1)) % ZS), left
        ref = gathered.at[s, q, :, shard]
        return remote(ref, ref, ring_send.at[s, q, way, k - 1], ring_recv.at[s, q, way, k - 1], where)

    def ring_landed(s, q, k, way):
        if way == 0:
            shard = slot_at((z + ZS - k) % ZS)
        else:
            shard = slot_at((z + k) % ZS)
        landed(gathered.at[s, q, :, shard], ring_recv.at[s, q, way, k - 1])

    def ring(s, k):
        if k == 1:
            landed(gathered.at[s, :, :, slot_at(z)], r_sem.at[s])
        for q in range(2):
            for way in range(2):
                if 1 < k < 5 or (k == 5 and way == q):
                    ring_landed(s, q, k - 1, way)
                if k < 4 or (k == 4 and way == q):
                    ring_copy(s, q, k, way).start()

    def separate(s, m):
        if m == 0:
            loads[s].wait()

        def body(i, carry):
            at = pl.multiple_of(i * 64, 64)
            for q in range(2):
                dense[s, m, q, pl.ds(at, 64), :] = raw[s, m, pl.ds(at, 64), q, :]
            return carry

        lax.fori_loop(0, 8, body, 0)

    def core_copy(s, m):
        return remote(
            term.at[s, m, :, 1 - core], other.at[s, m], core_send.at[s, m], core_recv.at[s, m], mate
        )

    def products(s):
        keep = [
            [-mask[s, m * ROWS + r, q * ROWS + c].astype(F32) for q in range(2)]
            for m in range(2)
        ]
        for m in range(2):
            def body(i, carry):
                at = pl.multiple_of(i * 256, 256)
                total = None
                for q in range(2):
                    right_side = gathered[s, q].reshape(512, 512)
                    part = keep[m][q] * jnp.dot(
                        dense[s, m, q, pl.ds(at, 256), :], right_side, preferred_element_type=F32
                    )
                    total = part if total is None else total + part
                term[s, m, pl.ds(i * 4, 4)] = total.reshape(4, 2, PIECE, 512)
                high = total.astype(BF16)
                split[m, 0, pl.ds(at, 256), :] = high
                split[m, 1, pl.ds(at, 256), :] = (total - high.astype(F32)).astype(BF16)
                return carry

            lax.fori_loop(0, 2, body, 0)
            core_copy(s, m).start()

    def t_copy(s, d):
        p = chip_peer(d)
        return remote(
            send_t.at[s, d - 1], recv_t.at[s, d - 1], t_sem.at[s, 0], t_sem.at[s, 1], (r, p * 2 + core)
        )

    def send_partials(s):
        for m in range(2):
            landed(other.at[s, m], core_recv.at[s, m])

        def body(d, carry):
            p = chip_peer(d)
            x = jnp.concatenate([term[s, m, p, core] + other[s, m, p] for m in range(2)], axis=0)
            pack_into(send_t.at[s, d - 1], x)
            t_copy(s, d).start()
            return carry

        lax.fori_loop(1, CHIPS, body, 0)
        for m in range(2):
            cols[s, m] = term[s, m, chip, core] + other[s, m, chip]

    def cols_copy(s):
        return pltpu.make_async_copy(cols.at[s], cols_out.at[s], c_sem.at[s])

    def sum_columns(s):
        landed(recv_t.at[s], t_sem.at[s, 1])

        def body(d, carry):
            cols[s] += unpack(recv_t.at[s, d], 64).reshape(2, PIECE, 512)
            return carry

        lax.fori_loop(0, CHIPS - 1, body, 0)
        cols_copy(s).start()

    def half_copy(s):
        return remote(own_g.at[s, 1 - core], other_g.at[s], d_sem.at[s, 0], d_sem.at[s, 1], mate)

    def diagonal_terms(s):
        landed(row_factor.at[s, :, :, 1 - core], m_sem.at[s, 3])
        for half in (1 - core, core):
            total = None
            for m in range(2):
                at = pl.multiple_of(half * 256, 256)
                left_side = row_factor[s, m, :, :, :, pl.ds(at, 256)].reshape(512, 256)
                for part in range(2):
                    dot = lax.dot_general(
                        left_side, split[m, part], (((0,), (0,)), ((), ())), preferred_element_type=F32
                    )
                    total = dot if total is None else total + dot
            own_g[s, half] = total
            if half is not core:
                half_copy(s).start()

    def g_copy(s, d):
        p = chip_peer(d)
        return remote(
            send_g.at[s, d - 1], recv_g.at[s, d - 1], g_sem.at[s, 0], g_sem.at[s, 1], (r, p * 2 + core)
        )

    def send_terms(s):
        landed(other_g.at[s], d_sem.at[s, 1])

        def body(d, carry):
            at = pl.multiple_of(chip_peer(d) * PIECE, PIECE)
            pack_into(send_g.at[s, d - 1], own_g[s, core, pl.ds(at, PIECE), :] + other_g[s, pl.ds(at, PIECE), :])
            g_copy(s, d).start()
            return carry

        lax.fori_loop(1, CHIPS, body, 0)

    def u_copy(s, d):
        return remote(
            tiles.at[s, row_peer(d)], recv_tiles.at[s, d - 1], u_sem.at[s, 0], u_sem.at[s, 1], (row_peer(d), c)
        )

    def send_tiles(s):
        landed(recv_g.at[s], g_sem.at[s, 1])
        own = pl.ds(pl.multiple_of(chip * PIECE, PIECE), PIECE)
        mine = own_g[s, core, own, :] + other_g[s, own, :]
        total = lax.fori_loop(0, CHIPS - 1, lambda d, x: x + unpack(recv_g.at[s, d], PIECE), mine)
        for i in range(4):
            for j in range(4):
                tiles[s, i * 4 + j] = total[i * 8 : i * 8 + 8, j * 128 : j * 128 + 128]

        def body(d, carry):
            u_copy(s, d).start()
            return carry

        lax.fori_loop(1, ROWS, body, 0)

    def f_copy(s, d):
        ref = final.at[s, r]
        return remote(ref, ref, f_sem.at[s, 0], f_sem.at[s, 1], (row_peer(d), c))

    def sum_tiles(s):
        landed(recv_tiles.at[s], u_sem.at[s, 1])
        final[s, r] = lax.fori_loop(0, ROWS - 1, lambda d, x: x + recv_tiles[s, d], tiles[s, r])

        def body(d, carry):
            f_copy(s, d).start()
            return carry

        lax.fori_loop(1, ROWS, body, 0)

    def h_copy(s, d):
        ref = packed.at[s, core, chip]
        return remote(ref, ref, h_sem.at[s, 0], h_sem.at[s, 1], (r, chip_peer(d) * 2 + core))

    def send_diagonal(s):
        landed(recv_tiles.at[s], f_sem.at[s, 1])
        rows = [jnp.concatenate([final[s, i * 4 + j] for j in range(4)], axis=1) for i in range(4)]
        pack_into(packed.at[s, core, chip], jnp.concatenate(rows, axis=0))

        def body(d, carry):
            h_copy(s, d).start()
            return carry

        lax.fori_loop(1, CHIPS, body, 0)

    def k_copy(s):
        ref = packed.at[s, core]
        return remote(ref, ref, k_sem.at[s, 0], k_sem.at[s, 1], mate)

    def share_diagonal(s):
        landed(recv_g.at[s], h_sem.at[s, 1])
        k_copy(s).start()

    def out_copy(s):
        return pltpu.make_async_copy(diag.at[s], diag_out.at[s], o_sem.at[s])

    def write_diagonal(s):
        landed(packed.at[s, 1 - core], k_sem.at[s, 1])

        def body(p, carry):
            for half in range(2):
                at = pl.multiple_of(half * 256 + p * PIECE, PIECE)
                diag[s, pl.ds(at, PIECE), :] = unpack(packed.at[s, half, p], PIECE)
            return carry

        lax.fori_loop(0, CHIPS, body, 0)
        out_copy(s).start()

    stage = {
        "D": separate, "P": forward_piece, "A": spread_rows, "F": share_rows, "R": ring,
        "1": products, "2": send_partials, "3": sum_columns, "4": diagonal_terms, "5": send_terms,
        "6": send_tiles, "7": sum_tiles, "8": send_diagonal, "9": share_diagonal, "W": write_diagonal,
    }
    order = (
        "D00", "P0", "A0", "D01", "P1", "A1", "R01", "P2", "A2", "R11", "D10", "R02",
        "D11", "R12", "F0", "R03", "R21", "D20", "R04", "R13", "R22", "D21", "F1", "R05",
        "10", "R14", "40", "R23", "R15", "50", "20", "R24", "F2", "11", "41", "R25",
        "51", "12", "42", "52", "21", "60", "22", "30", "61", "70", "31", "62",
        "71", "80", "72", "81", "90", "32", "82", "91", "W0", "92", "W1", "W2",
    )
    for word in order:
        stage[word[0]](*(int(n) for n in word[1:]))

    for s in range(NODES):

        @pl.when(shift != 0)
        def _():
            first_hop(s).wait_send()

        @pl.when(c != target)
        def _():
            second_hop(s, 0).wait_send()

        second_hop(s, 1).wait_send()
        landed(row_factor.at[s, :, pl.ds(0, CHIPS - 1), core], m_sem.at[s, 0])
        rows_copy(s).wait_send()
        for q in range(2):
            for k in range(1, 5):
                for way in range(2):
                    if k < 4 or way == q:
                        ring_copy(s, q, k, way).wait_send()
        for m in range(2):
            core_copy(s, m).wait_send()
        half_copy(s).wait_send()
        landed(send_t.at[s], t_sem.at[s, 0])
        landed(send_g.at[s], g_sem.at[s, 0])
        landed(recv_tiles.at[s], u_sem.at[s, 0])
        landed(recv_tiles.at[s], f_sem.at[s, 0])
        landed(recv_g.at[s], h_sem.at[s, 0])
        k_copy(s).wait_send()
        cols_copy(s).wait()
        out_copy(s).wait()


def shards(inverse_blocks, factor_cols, diag_inverse, block_mask):
    blocks = inverse_blocks.reshape(NODES, 2, 512, 2, 512)
    factor = factor_cols.reshape(NODES, 2, PIECE, 512)
    vmem = pltpu.VMEM
    dma = pltpu.SemaphoreType.DMA
    columns, term = pl.pallas_call(
        kernel,
        out_shape=(
            jax.ShapeDtypeStruct((NODES, 2, PIECE, 512), F32),
            jax.ShapeDtypeStruct((NODES, 512, 512), F32),
        ),
        in_specs=[
            pl.BlockSpec(memory_space=pl.ANY),
            pl.BlockSpec(memory_space=pl.ANY),
            pl.BlockSpec(memory_space=pltpu.SMEM),
        ],
        out_specs=(
            pl.BlockSpec(memory_space=pl.ANY),
            pl.BlockSpec(memory_space=pl.ANY),
        ),
        scratch_shapes=[
            vmem((NODES, 2, 512, 2, 512), BF16),
            vmem((NODES, 2, 2, 512, 512), BF16),
            vmem((NODES, 2, PIECE, 512), BF16),
            vmem((NODES, 2, PIECE, 512), BF16),
            vmem((NODES, 2, 2, ZS, PIECE, 512), BF16),
            vmem((NODES, 2, CHIPS, 2, PIECE, 512), BF16),
            vmem((NODES, 2, CHIPS, 2, PIECE, 512), F32),
            vmem((2, 2, 512, 512), BF16),
            vmem((NODES, 2, CHIPS, PIECE, 512), F32),
            vmem((NODES, CHIPS - 1, T_WORDS, 128), I32),
            vmem((NODES, CHIPS - 1, T_WORDS, 128), I32),
            vmem((NODES, 2, PIECE, 512), F32),
            vmem((NODES, 2, 256, 512), F32),
            vmem((NODES, 256, 512), F32),
            vmem((NODES, CHIPS - 1, G_WORDS, 128), I32),
            vmem((NODES, CHIPS - 1, G_WORDS, 128), I32),
            vmem((NODES, ROWS, 8, 128), F32),
            vmem((NODES, ROWS - 1, 8, 128), F32),
            vmem((NODES, ROWS, 8, 128), F32),
            vmem((NODES, 2, CHIPS, G_WORDS, 128), I32),
            vmem((NODES, 512, 512), F32),
            dma((NODES,)),
            dma((1,)),
            dma((NODES, 2)),
            dma((NODES, 2)),
            dma((NODES,)),
            dma((NODES, 4)),
            dma((NODES, 2, 2, 4)),
            dma((NODES, 2, 2, 4)),
            dma((NODES, 2)),
            dma((NODES, 2)),
            dma((NODES, 2)),
            dma((NODES,)),
            dma((NODES, 2)),
            dma((NODES, 2)),
            dma((NODES, 2)),
            dma((NODES, 2)),
            dma((NODES, 2)),
            dma((NODES, 2)),
            dma((NODES,)),
        ],
        compiler_params=pltpu.CompilerParams(
            collective_id=0, has_side_effects=True, vmem_limit_bytes=48 * 2**20
        ),
        cost_estimate=pl.CostEstimate(
            flops=NODES * 4 * 2 * 512**3, bytes_accessed=16 * 2**20, transcendentals=0
        ),
    )(blocks, factor, block_mask)
    inverse_cols = columns.reshape(NODES, 2, 1, PIECE, 512)
    return (inverse_cols, diag_inverse - term)


def solution(mesh):
    placed = (
        P(None, None, "prow", None, None, "pcol", None),
        P(None, None, "prow", "pcol", None),
        P(),
        P(),
    )
    return jax.shard_map(
        shards,
        mesh=mesh,
        in_specs=placed,
        out_specs=(P(None, None, "prow", "pcol", None), P()),
        check_vma=False,
    )
```

```python
import jax
import jax.numpy as jnp
from jax import lax
from jax.experimental import pallas as pl
from jax.experimental.pallas import tpu as pltpu
from jax.sharding import PartitionSpec as P

MESH = pl.DeviceIdType.MESH
F32 = jnp.float32
BF16 = jnp.bfloat16
I32 = jnp.int32

NODES = 3
ZS = 8
YS = 4
CHIPS = 8
ROWS = 16
PLANE = 16
FIRST = 0
PIECE = 32
T_WORDS = 136
G_WORDS = 40


def scale_of(code):
    value = code.astype(F32)
    return jnp.where(code > 0, value * (2.0**-8), value * (-(2.0**-30)))


def code_of(top):
    coarse = jnp.ceil(top * 256.0).astype(I32)
    fine = -jnp.maximum(jnp.ceil(jnp.minimum(top, 1.0) * (2.0**30)), 1.0).astype(I32)
    return jnp.where(top >= 1.0, coarse, fine)


def largest(x):
    return jnp.max(jnp.max(jnp.abs(x), axis=0, keepdims=True), axis=1, keepdims=True)


def pack_into(ref, x, code):
    rows = x.shape[0]
    inverse = 32767.0 / scale_of(code)
    q = jnp.floor(x * inverse + 0.5).astype(I32)
    for half in range(2):
        upper = q[:, half * 128 : half * 128 + 128]
        lower = q[:, 256 + half * 128 : 384 + half * 128]
        ref[half * rows : half * rows + rows, :] = (upper << 16) | (lower & 0xFFFF)
    ref[2 * rows : 2 * rows + 8, :] = jnp.broadcast_to(code, (8, 128))


def unpack(ref, rows):
    step = scale_of(ref[2 * rows : 2 * rows + 8, :])[0:1, :] * (1.0 / 32767.0)
    parts = []
    words = [ref[half * rows : half * rows + rows, :] for half in range(2)]
    for word in words:
        parts.append((word >> 16).astype(F32) * step)
    for word in words:
        parts.append(((word << 16) >> 16).astype(F32) * step)
    return jnp.concatenate(parts, axis=1)


def kernel(
    blocks, factor_in, mask_in, cols_out, diag_out,
    raw, dense, factor, middle, column, gathered, row_factor, term, split, other, send_t, recv_t, cols,
    own_g, other_g, send_g, recv_g, levels, packed, diag, mask,
    a_sem, l_sem, p_sem, q_sem, r_sem, z_sem, y_sem, m_sem, ring_send, ring_recv, core_send, core_recv,
    t_sem, c_sem, d_sem, g_sem, u_sem, h_sem, k_sem, o_sem,
):
    r = lax.axis_index("prow")
    c = lax.axis_index("pcol")
    x_lo, z = r // ZS, r % ZS
    x_hi, y, core = c // (2 * YS), (c // 2) % YS, c % 2
    chip = c // 2
    mate = (r, chip * 2 + (1 - core))
    shift = y + YS * core
    origin = (z + ZS - shift) % ZS
    target = x_lo * ZS + origin

    def slot_at(where):
        gap = (where + ZS - c % ZS) % ZS
        return (gap % YS) * 2 + gap // YS

    def z_peer(d):
        j = d - 1
        step = 4 + j // 2 - (j % 2) * (2 * (j // 2) + 1)
        return x_lo * ZS + (z + step + ZS) % ZS

    place_here = (x_lo * 2 + x_hi) * YS + y

    def plane_peer(d):
        i, j = (d - 1) % 4, (d - 1) // 4
        step = 2 + j // 2 - (j % 2) * (2 * (j // 2) + 1)
        return (x_lo + (i + 1) // 2) % 2, (x_hi + 1 - i // 2) % 2, (y + step + YS) % YS

    def plane_device(d):
        lo, hi, at_y = plane_peer(d)
        return (lo * ZS + z, hi * (2 * YS) + at_y * 2 + core)

    def plane_place(d):
        lo, hi, at_y = plane_peer(d)
        return (lo * 2 + hi) * YS + at_y

    def chip_peer(d):
        j = (d - 1) // 2
        step = 2 + j // 2 - (j % 2) * (2 * (j // 2) + 1)
        return ((x_hi + d % 2) % 2) * YS + (y + step + YS) % YS

    def remote(src, dst, send, recv, where):
        return pltpu.make_async_remote_copy(
            src_ref=src, dst_ref=dst, send_sem=send, recv_sem=recv, device_id=where, device_id_type=MESH
        )

    def landed(ref, sem):
        pltpu.make_async_copy(ref, ref, sem).wait()

    own_load = pltpu.make_async_copy(factor_in, factor, l_sem.at[0])
    own_load.start()
    mask_load = pltpu.make_async_copy(mask_in, mask, l_sem.at[1])
    mask_load.start()
    loads = [
        pltpu.make_async_copy(blocks.at[s], raw.at[s], a_sem.at[s]) for s in range(NODES)
    ]
    for load in loads:
        load.start()

    barrier = pltpu.get_barrier_semaphore()

    def greet(where):
        pl.semaphore_signal(barrier, inc=1, device_id=where, device_id_type=MESH)

    same_lo = (r, target)
    other_lo = ((r + ZS) % ROWS, target)
    has_self = c == target if FIRST == 0 else c // ZS == x_lo
    rounds = 1 if FIRST == 0 else ZS

    def greet_plane(i, carry):
        for lo in range(2):
            if FIRST == 0:
                there = (lo * ZS + z, target)
                back = ((c // ZS) * ZS + z, lo * ZS + slot_at(z))
            else:
                there = (lo * ZS + z, x_lo * ZS + i)
                back = ((c // ZS) * ZS + z, lo * ZS + i)

            @pl.when(jnp.logical_not(jnp.logical_and(there[0] == r, there[1] == c)))
            def _():
                greet(there)

            @pl.when(jnp.logical_not(jnp.logical_and(back[0] == r, back[1] == c)))
            def _():
                greet(back)

        return carry

    lax.fori_loop(0, rounds, greet_plane, 0)
    greet(mate)

    def greet_z(d, carry):
        greet((z_peer(d), c))
        return carry

    lax.fori_loop(1, ZS, greet_z, 0)

    def greet_xy(d, carry):
        greet(plane_device(d))
        return carry

    lax.fori_loop(1, PLANE, greet_xy, 0)
    own_load.wait()

    partners = 4 * rounds + 1 + (ZS - 1) + (PLANE - 1)

    @pl.when(jnp.logical_not(has_self))
    def _():
        pl.semaphore_wait(barrier, partners)

    @pl.when(has_self)
    def _():
        pl.semaphore_wait(barrier, partners - 2)

    def first_hop(s):
        where = (x_lo * ZS + (z + shift) % ZS, c)
        return remote(factor.at[s], middle.at[s], p_sem.at[s, 0], p_sem.at[s, 1], where)

    right = (x_lo * ZS + (z + 1) % ZS, c)
    left = (x_lo * ZS + (z + ZS - 1) % ZS, c)

    def column_copy(k, way):
        if way == 0:
            begun, where = (z + ZS - (k - 1)) % ZS, right
        else:
            begun, where = (z + (k - 1)) % ZS, left
        ref = column.at[begun] if k < 4 else column.at[begun, way]
        src = ref if k > 1 else factor.at[0]
        return remote(src, ref, z_sem.at[0, way, k - 1], z_sem.at[1, way, k - 1], where)

    def column_landed(k, way):
        begun = (z + ZS - k) % ZS if way == 0 else (z + k) % ZS
        landed(column.at[begun] if k < 4 else column.at[begun, way], z_sem.at[1, way, k - 1])

    def place_copy(i, lo):
        begun = (z + i) % ZS
        src = factor.at[0] if i == 0 else column.at[begun]
        where = (((x_lo + lo) % 2) * ZS + z, x_lo * ZS + begun)
        return remote(src, gathered.at[0, :, c // ZS, c % ZS], y_sem.at[i, lo], r_sem.at[0], where)

    def place(i):
        begun = (z + i) % ZS
        place_copy(i, 1).start()

        @pl.when(c != x_lo * ZS + begun)
        def _():
            place_copy(i, 0).start()

        @pl.when(c == x_lo * ZS + begun)
        def _():
            src = factor.at[0] if i == 0 else column.at[begun]
            pltpu.make_async_copy(src, gathered.at[0, :, c // ZS, c % ZS], r_sem.at[0]).start()

    def around(k):
        for way in range(2):
            if k > 1:
                column_landed(k - 1, way)
            if k < 5:
                column_copy(k, way).start()
        if k == 1:
            place(0)
        elif k < 5:
            place(ZS - (k - 1))
            place(k - 1)
        else:
            place(4)

    if FIRST:
        around(1)
    for s in range(FIRST, NODES):

        @pl.when(shift != 0)
        def _():
            first_hop(s).start()

        @pl.when(shift == 0)
        def _():
            pltpu.make_async_copy(factor.at[s], middle.at[s], p_sem.at[s, 1]).start()

    def second_hop(s, way):
        where = same_lo if way == 0 else other_lo
        return remote(
            middle.at[s], gathered.at[s, :, c // ZS, c % ZS], q_sem.at[s, way], r_sem.at[s], where
        )

    def forward_piece(s):
        landed(middle.at[s], p_sem.at[s, 1])
        second_hop(s, 1).start()

        @pl.when(c != target)
        def _():
            second_hop(s, 0).start()

        @pl.when(c == target)
        def _():
            pltpu.make_async_copy(middle.at[s], gathered.at[s, :, c // ZS, c % ZS], r_sem.at[s]).start()

    across = (r, ((x_hi + 1) % 2) * (2 * YS) + y * 2 + core)

    def across_copy(s):
        return remote(
            factor.at[s], row_factor.at[s, x_hi, y, core], m_sem.at[s, 0], m_sem.at[s, 1], across
        )

    def cross_rows(s):
        across_copy(s).start()
        row_factor[s, x_hi, y, core] = factor[s]

    def row_copy(s, d):
        ref = row_factor.at[s, :, y, core]
        where = (r, x_hi * (2 * YS) + ((y + d) % YS) * 2 + core)
        return remote(ref, ref, m_sem.at[s, 2], m_sem.at[s, 3], where)

    def spread_rows(s):
        landed(row_factor.at[s, 1 - x_hi, y, core], m_sem.at[s, 1])
        for d in (2, 1, 3):
            row_copy(s, d).start()

    def rows_copy(s):
        ref = row_factor.at[s, :, :, core]
        return remote(ref, ref, m_sem.at[s, 4], m_sem.at[s, 5], mate)

    def share_rows(s):
        landed(row_factor.at[s, :, pl.ds(0, YS - 1), core], m_sem.at[s, 3])
        rows_copy(s).start()

    def ring_copy(s, q, k, way):
        if way == 0:
            shard, where = slot_at((z + ZS - (k - 1)) % ZS), right
        else:
            shard, where = slot_at((z + (k - 1)) % ZS), left
        ref = gathered.at[s, q, :, shard]
        return remote(ref, ref, ring_send.at[s, q, way, k - 1], ring_recv.at[s, q, way, k - 1], where)

    def ring_landed(s, q, k, way):
        if way == 0:
            shard = slot_at((z + ZS - k) % ZS)
        else:
            shard = slot_at((z + k) % ZS)
        landed(gathered.at[s, q, :, shard], ring_recv.at[s, q, way, k - 1])

    def ring(s, k):
        if k == 1:
            landed(gathered.at[s, :, :, slot_at(z)], r_sem.at[s])
        for q in range(2):
            for way in range(2):
                if 1 < k < 5 or (k == 5 and way == q):
                    ring_landed(s, q, k - 1, way)
                if k < 4 or (k == 4 and way == q):
                    ring_copy(s, q, k, way).start()

    def separate(s, m):
        if m == 0:
            loads[s].wait()

        def body(i, carry):
            at = pl.multiple_of(i * 64, 64)
            for q in range(2):
                dense[s, m, q, pl.ds(at, 64), :] = raw[s, m, pl.ds(at, 64), q, :]
            return carry

        lax.fori_loop(0, 8, body, 0)

    def core_copy(s, m):
        return remote(
            term.at[s, m, :, 1 - core], other.at[s, m], core_send.at[s, m], core_recv.at[s, m], mate
        )

    def products(s):
        if s < FIRST:
            landed(gathered.at[0], r_sem.at[0])
        if s == 0:
            mask_load.wait()
        keep = [
            [-mask[s, m * ROWS + r, q * ROWS + c].astype(F32) for q in range(2)]
            for m in range(2)
        ]
        for m in range(2):
            def body(i, carry):
                at = pl.multiple_of(i * 256, 256)
                total = None
                for q in range(2):
                    right_side = gathered[s, q].reshape(512, 512)
                    part = keep[m][q] * jnp.dot(
                        dense[s, m, q, pl.ds(at, 256), :], right_side, preferred_element_type=F32
                    )
                    total = part if total is None else total + part
                term[s, m, pl.ds(i * 4, 4)] = total.reshape(4, 2, PIECE, 512)
                high = total.astype(BF16)
                split[m, 0, pl.ds(at, 256), :] = high
                split[m, 1, pl.ds(at, 256), :] = (total - high.astype(F32)).astype(BF16)
                return carry

            lax.fori_loop(0, 2, body, 0)
            core_copy(s, m).start()

    def t_copy(s, d):
        p = chip_peer(d)
        return remote(
            send_t.at[s, d - 1], recv_t.at[s, d - 1], t_sem.at[s, 0], t_sem.at[s, 1], (r, p * 2 + core)
        )

    def send_partials(s):
        for m in range(2):
            landed(other.at[s, m], core_recv.at[s, m])

        def join(p, top):
            for m in range(2):
                x = term[s, m, p, core] + other[s, m, p]
                term[s, m, p, core] = x
                top = jnp.maximum(top, jnp.abs(x))
            return top

        code = code_of(largest(lax.fori_loop(0, CHIPS, join, jnp.zeros((PIECE, 512), F32))))

        def body(d, carry):
            p = chip_peer(d)
            x = jnp.concatenate([term[s, m, p, core] for m in range(2)], axis=0)
            pack_into(send_t.at[s, d - 1], x, code)
            t_copy(s, d).start()
            return carry

        lax.fori_loop(1, CHIPS, body, 0)
        for m in range(2):
            cols[s, m] = term[s, m, chip, core]

    def cols_copy(s):
        return pltpu.make_async_copy(cols.at[s], cols_out.at[s], c_sem.at[s])

    def sum_columns(s):
        landed(recv_t.at[s], t_sem.at[s, 1])

        def body(d, carry):
            cols[s] += unpack(recv_t.at[s, d], 64).reshape(2, PIECE, 512)
            return carry

        lax.fori_loop(0, CHIPS - 1, body, 0)
        cols_copy(s).start()

    def half_copy(s):
        return remote(own_g.at[s, 1 - core], other_g.at[s], d_sem.at[s, 0], d_sem.at[s, 1], mate)

    def diagonal_terms(s):
        landed(row_factor.at[s, :, :, 1 - core], m_sem.at[s, 5])
        for half in (1 - core, core):
            total = None
            for m in range(2):
                at = pl.multiple_of(half * 256, 256)
                left_side = row_factor[s, :, :, :, m, :, pl.ds(at, 256)].reshape(512, 256)
                for part in range(2):
                    dot = lax.dot_general(
                        left_side, split[m, part], (((0,), (0,)), ((), ())), preferred_element_type=F32
                    )
                    total = dot if total is None else total + dot
            own_g[s, half] = total
            if half is not core:
                half_copy(s).start()

    def g_copy(s, d):
        return remote(
            send_g.at[s, d - 1], recv_g.at[s, d - 1], g_sem.at[s, 0], g_sem.at[s, 1], plane_device(d)
        )

    def send_terms(s):
        landed(other_g.at[s], d_sem.at[s, 1])
        whole = own_g[s, core] + other_g[s]
        own_g[s, core] = whole
        code = code_of(largest(whole))

        def body(d, carry):
            at = pl.multiple_of(plane_place(d) * 16, 16)
            pack_into(send_g.at[s, d - 1], own_g[s, core, pl.ds(at, 16), :], code)
            g_copy(s, d).start()
            return carry

        lax.fori_loop(1, PLANE, body, 0)

    def u_copy(s, d):
        ref = levels.at[s, z]
        return remote(ref, ref, u_sem.at[s, 0], u_sem.at[s, 1], (z_peer(d), c))

    def send_levels(s):
        landed(recv_g.at[s], g_sem.at[s, 1])
        mine = own_g[s, core, pl.ds(pl.multiple_of(place_here * 16, 16), 16), :]
        total = lax.fori_loop(0, PLANE - 1, lambda d, x: x + unpack(recv_g.at[s, d], 16), mine)
        pack_into(levels.at[s, z], total, code_of(largest(total)))

        def body(d, carry):
            u_copy(s, d).start()
            return carry

        lax.fori_loop(1, ZS, body, 0)

    def h_copy(s, d):
        ref = packed.at[s, core, place_here]
        return remote(ref, ref, h_sem.at[s, 0], h_sem.at[s, 1], plane_device(d))

    def send_diagonal(s):
        landed(levels.at[s, pl.ds(0, ZS - 1)], u_sem.at[s, 1])
        zero = jnp.zeros((16, 512), F32)
        total = lax.fori_loop(0, ZS, lambda i, x: x + unpack(levels.at[s, i], 16), zero)
        pack_into(packed.at[s, core, place_here], total, code_of(largest(total)))

        def body(d, carry):
            h_copy(s, d).start()
            return carry

        lax.fori_loop(1, PLANE, body, 0)

    def k_copy(s):
        ref = packed.at[s, core]
        return remote(ref, ref, k_sem.at[s, 0], k_sem.at[s, 1], mate)

    def share_diagonal(s):
        landed(recv_g.at[s], h_sem.at[s, 1])
        k_copy(s).start()

    def out_copy(s):
        return pltpu.make_async_copy(diag.at[s], diag_out.at[s], o_sem.at[s])

    def write_diagonal(s):
        landed(packed.at[s, 1 - core], k_sem.at[s, 1])

        def body(p, carry):
            for half in range(2):
                at = pl.multiple_of(half * 256 + p * 16, 16)
                diag[s, pl.ds(at, 16), :] = unpack(packed.at[s, half, p], 16)
            return carry

        lax.fori_loop(0, PLANE, body, 0)
        out_copy(s).start()

    stage = {
        "D": separate, "Z": around, "P": forward_piece, "B": cross_rows, "A": spread_rows, "F": share_rows, "R": ring,
        "1": products, "2": send_partials, "3": sum_columns, "4": diagonal_terms, "5": send_terms,
        "6": send_levels, "7": send_diagonal, "8": share_diagonal, "9": write_diagonal,
    }
    order = (
        "B0", "B1", "B2", "D00", "D01", "P0", "A0", "D10", "P1", "D11", "R01", "A1",
        "P2", "D20", "R02", "R11", "D21", "R03", "R12", "A2", "F0", "R04", "R13", "F1",
        "R05", "R14", "10", "R21", "40", "F2", "R15", "R22", "20", "50", "11", "R23",
        "R24", "21", "41", "51", "60", "R25", "12", "42", "52", "70", "61", "30",
        "62", "22", "80", "71", "72", "31", "81", "90", "82", "91", "32", "92",
    )
    for word in order:
        stage[word[0]](*(int(n) for n in word[1:]))

    if FIRST:
        for k in range(1, 5):
            for way in range(2):
                column_copy(k, way).wait_send()
        for i in range(ZS):
            place_copy(i, 1).wait_send()

            @pl.when(c != x_lo * ZS + (z + i) % ZS)
            def _():
                place_copy(i, 0).wait_send()

    for s in range(NODES):
        if s >= FIRST:

            @pl.when(shift != 0)
            def _():
                first_hop(s).wait_send()

            @pl.when(c != target)
            def _():
                second_hop(s, 0).wait_send()

            second_hop(s, 1).wait_send()
            for q in range(2):
                for k in range(1, 5):
                    for way in range(2):
                        if k < 4 or way == q:
                            ring_copy(s, q, k, way).wait_send()
        across_copy(s).wait_send()
        landed(row_factor.at[s, :, pl.ds(0, YS - 1), core], m_sem.at[s, 2])
        rows_copy(s).wait_send()
        for m in range(2):
            core_copy(s, m).wait_send()
        half_copy(s).wait_send()
        landed(send_t.at[s], t_sem.at[s, 0])
        landed(send_g.at[s], g_sem.at[s, 0])
        landed(levels.at[s, pl.ds(0, ZS - 1)], u_sem.at[s, 0])
        landed(recv_g.at[s], h_sem.at[s, 0])
        k_copy(s).wait_send()
        cols_copy(s).wait()
        out_copy(s).wait()


def shards(inverse_blocks, factor_cols, diag_inverse, block_mask):
    blocks = inverse_blocks.reshape(NODES, 2, 512, 2, 512)
    factor = factor_cols.reshape(NODES, 2, PIECE, 512)
    vmem = pltpu.VMEM
    dma = pltpu.SemaphoreType.DMA
    columns, term = pl.pallas_call(
        kernel,
        out_shape=(
            jax.ShapeDtypeStruct((NODES, 2, PIECE, 512), F32),
            jax.ShapeDtypeStruct((NODES, 512, 512), F32),
        ),
        in_specs=[
            pl.BlockSpec(memory_space=pltpu.HBM),
            pl.BlockSpec(memory_space=pltpu.HBM),
            pl.BlockSpec(memory_space=pltpu.HBM),
        ],
        out_specs=(
            pl.BlockSpec(memory_space=pl.ANY),
            pl.BlockSpec(memory_space=pl.ANY),
        ),
        scratch_shapes=[
            vmem((NODES, 2, 512, 2, 512), BF16),
            vmem((NODES, 2, 2, 512, 512), BF16),
            vmem((NODES, 2, PIECE, 512), BF16),
            vmem((NODES, 2, PIECE, 512), BF16),
            vmem((ZS, 2, PIECE, 512), BF16),
            vmem((NODES, 2, 2, ZS, PIECE, 512), BF16),
            vmem((NODES, 2, YS, 2, 2, PIECE, 512), BF16),
            vmem((NODES, 2, CHIPS, 2, PIECE, 512), F32),
            vmem((2, 2, 512, 512), BF16),
            vmem((NODES, 2, CHIPS, PIECE, 512), F32),
            vmem((NODES, CHIPS - 1, T_WORDS, 128), I32),
            vmem((NODES, CHIPS - 1, T_WORDS, 128), I32),
            vmem((NODES, 2, PIECE, 512), F32),
            vmem((NODES, 2, 256, 512), F32),
            vmem((NODES, 256, 512), F32),
            vmem((NODES, PLANE - 1, G_WORDS, 128), I32),
            vmem((NODES, PLANE - 1, G_WORDS, 128), I32),
            vmem((NODES, ZS, G_WORDS, 128), I32),
            vmem((NODES, 2, PLANE, G_WORDS, 128), I32),
            vmem((NODES, 512, 512), F32),
            pltpu.SMEM((NODES, 32, 32), I32),
            dma((NODES,)),
            dma((2,)),
            dma((NODES, 2)),
            dma((NODES, 2)),
            dma((NODES,)),
            dma((2, 2, 4)),
            dma((ZS, 2)),
            dma((NODES, 6)),
            dma((NODES, 2, 2, 4)),
            dma((NODES, 2, 2, 4)),
            dma((NODES, 2)),
            dma((NODES, 2)),
            dma((NODES, 2)),
            dma((NODES,)),
            dma((NODES, 2)),
            dma((NODES, 2)),
            dma((NODES, 2)),
            dma((NODES, 2)),
            dma((NODES, 2)),
            dma((NODES,)),
        ],
        compiler_params=pltpu.CompilerParams(
            collective_id=0, has_side_effects=True, vmem_limit_bytes=48 * 2**20
        ),
        cost_estimate=pl.CostEstimate(
            flops=NODES * 4 * 2 * 512**3, bytes_accessed=16 * 2**20, transcendentals=0
        ),
    )(blocks, factor, block_mask)
    inverse_cols = columns.reshape(NODES, 2, 1, PIECE, 512)
    return (inverse_cols, diag_inverse - term)


def solution(mesh):
    placed = (
        P(None, None, "prow", None, None, "pcol", None),
        P(None, None, "prow", "pcol", None),
        P(),
        P(),
    )
    return jax.shard_map(
        shards,
        mesh=mesh,
        in_specs=placed,
        out_specs=(P(None, None, "prow", "pcol", None), P()),
        check_vma=False,
    )
```

```python
import jax
import jax.numpy as jnp
from jax import lax
from jax.experimental import pallas as pl
from jax.experimental.pallas import tpu as pltpu
from jax.sharding import PartitionSpec as P

MESH = pl.DeviceIdType.MESH
F32 = jnp.float32
BF16 = jnp.bfloat16
I32 = jnp.int32

NODES = 3
ZS = 8
YS = 4
CHIPS = 8
ROWS = 16
PLANE = 16
FIRST = 0
SHARED = (1,)
PIECE = 32
T_WORDS = 136
G_WORDS = 40


def scale_of(code):
    value = code.astype(F32)
    return jnp.where(code > 0, value * (2.0**-8), value * (-(2.0**-30)))


def code_of(top):
    coarse = jnp.ceil(top * 256.0).astype(I32)
    fine = -jnp.maximum(jnp.ceil(jnp.minimum(top, 1.0) * (2.0**30)), 1.0).astype(I32)
    return jnp.where(top >= 1.0, coarse, fine)


def largest(x):
    return jnp.max(jnp.max(jnp.abs(x), axis=0, keepdims=True), axis=1, keepdims=True)


def pack_into(ref, x, code):
    rows = x.shape[0]
    inverse = 32767.0 / scale_of(code)
    q = jnp.floor(x * inverse + 0.5).astype(I32)
    for half in range(2):
        upper = q[:, half * 128 : half * 128 + 128]
        lower = q[:, 256 + half * 128 : 384 + half * 128]
        ref[half * rows : half * rows + rows, :] = (upper << 16) | (lower & 0xFFFF)
    ref[2 * rows : 2 * rows + 8, :] = jnp.broadcast_to(code, (8, 128))


def unpack(ref, rows):
    step = scale_of(ref[2 * rows : 2 * rows + 8, :])[0:1, :] * (1.0 / 32767.0)
    parts = []
    words = [ref[half * rows : half * rows + rows, :] for half in range(2)]
    for word in words:
        parts.append((word >> 16).astype(F32) * step)
    for word in words:
        parts.append(((word << 16) >> 16).astype(F32) * step)
    return jnp.concatenate(parts, axis=1)


def kernel(
    blocks, factor_in, mask_in, cols_out, diag_out,
    raw, dense, factor, middle, column, gathered, row_factor, term, split, other, send_t, recv_t, cols,
    own_g, other_g, send_g, recv_g, levels, packed, diag, mask,
    a_sem, l_sem, p_sem, q_sem, r_sem, x_sem, z_sem, y_sem, m_sem, ring_send, ring_recv, core_send, core_recv,
    t_sem, c_sem, d_sem, g_sem, u_sem, h_sem, k_sem, o_sem,
):
    r = lax.axis_index("prow")
    c = lax.axis_index("pcol")
    x_lo, z = r // ZS, r % ZS
    x_hi, y, core = c // (2 * YS), (c // 2) % YS, c % 2
    chip = c // 2
    mate = (r, chip * 2 + (1 - core))
    shift = y + YS * core
    origin = (z + ZS - shift) % ZS
    target = x_lo * ZS + origin

    def slot_at(where):
        gap = (where + ZS - c % ZS) % ZS
        return (gap % YS) * 2 + gap // YS

    def z_peer(d):
        j = d - 1
        step = 4 + j // 2 - (j % 2) * (2 * (j // 2) + 1)
        return x_lo * ZS + (z + step + ZS) % ZS

    place_here = (x_lo * 2 + x_hi) * YS + y

    def plane_peer(d):
        i, j = (d - 1) % 4, (d - 1) // 4
        step = 2 + j // 2 - (j % 2) * (2 * (j // 2) + 1)
        return (x_lo + (i + 1) // 2) % 2, (x_hi + 1 - i // 2) % 2, (y + step + YS) % YS

    def plane_device(d):
        lo, hi, at_y = plane_peer(d)
        return (lo * ZS + z, hi * (2 * YS) + at_y * 2 + core)

    def plane_place(d):
        lo, hi, at_y = plane_peer(d)
        return (lo * 2 + hi) * YS + at_y

    def chip_peer(d):
        j = (d - 1) // 2
        step = 2 + j // 2 - (j % 2) * (2 * (j // 2) + 1)
        return ((x_hi + d % 2) % 2) * YS + (y + step + YS) % YS

    def remote(src, dst, send, recv, where):
        return pltpu.make_async_remote_copy(
            src_ref=src, dst_ref=dst, send_sem=send, recv_sem=recv, device_id=where, device_id_type=MESH
        )

    def landed(ref, sem):
        pltpu.make_async_copy(ref, ref, sem).wait()

    own_load = pltpu.make_async_copy(factor_in, factor, l_sem.at[0])
    own_load.start()
    mask_load = pltpu.make_async_copy(mask_in, mask, l_sem.at[1])
    mask_load.start()
    loads = [
        pltpu.make_async_copy(blocks.at[s], raw.at[s], a_sem.at[s]) for s in range(NODES)
    ]
    for load in loads:
        load.start()

    barrier = pltpu.get_barrier_semaphore()

    def greet(where):
        pl.semaphore_signal(barrier, inc=1, device_id=where, device_id_type=MESH)

    same_lo = (r, target)
    other_lo = ((r + ZS) % ROWS, target)
    has_self = c == target if FIRST == 0 else c // ZS == x_lo
    rounds = 1 if FIRST == 0 else ZS

    def greet_plane(i, carry):
        for lo in range(2):
            if FIRST == 0:
                there = (lo * ZS + z, target)
                back = ((c // ZS) * ZS + z, lo * ZS + slot_at(z))
            else:
                there = (lo * ZS + z, x_lo * ZS + i)
                back = ((c // ZS) * ZS + z, lo * ZS + i)

            @pl.when(jnp.logical_not(jnp.logical_and(there[0] == r, there[1] == c)))
            def _():
                greet(there)

            @pl.when(jnp.logical_not(jnp.logical_and(back[0] == r, back[1] == c)))
            def _():
                greet(back)

        return carry

    lax.fori_loop(0, rounds, greet_plane, 0)
    greet(mate)

    def greet_z(d, carry):
        greet((z_peer(d), c))
        return carry

    lax.fori_loop(1, ZS, greet_z, 0)

    def greet_xy(d, carry):
        greet(plane_device(d))
        return carry

    lax.fori_loop(1, PLANE, greet_xy, 0)
    own_load.wait()

    partners = 4 * rounds + 1 + (ZS - 1) + (PLANE - 1)

    @pl.when(jnp.logical_not(has_self))
    def _():
        pl.semaphore_wait(barrier, partners)

    @pl.when(has_self)
    def _():
        pl.semaphore_wait(barrier, partners - 2)

    def first_hop(s):
        where = (x_lo * ZS + (z + shift) % ZS, c)
        return remote(factor.at[s], middle.at[s], p_sem.at[s, 0], p_sem.at[s, 1], where)

    right = (x_lo * ZS + (z + 1) % ZS, c)
    left = (x_lo * ZS + (z + ZS - 1) % ZS, c)

    def column_copy(k, way):
        if way == 0:
            begun, where = (z + ZS - (k - 1)) % ZS, right
        else:
            begun, where = (z + (k - 1)) % ZS, left
        ref = column.at[begun] if k < 4 else column.at[begun, way]
        src = ref if k > 1 else factor.at[0]
        return remote(src, ref, z_sem.at[0, way, k - 1], z_sem.at[1, way, k - 1], where)

    def column_landed(k, way):
        begun = (z + ZS - k) % ZS if way == 0 else (z + k) % ZS
        landed(column.at[begun] if k < 4 else column.at[begun, way], z_sem.at[1, way, k - 1])

    def place_copy(i, lo):
        begun = (z + i) % ZS
        src = factor.at[0] if i == 0 else column.at[begun]
        where = (((x_lo + lo) % 2) * ZS + z, x_lo * ZS + begun)
        return remote(src, gathered.at[0, :, c // ZS, c % ZS], y_sem.at[i, lo], r_sem.at[0], where)

    def place(i):
        begun = (z + i) % ZS
        place_copy(i, 1).start()

        @pl.when(c != x_lo * ZS + begun)
        def _():
            place_copy(i, 0).start()

        @pl.when(c == x_lo * ZS + begun)
        def _():
            src = factor.at[0] if i == 0 else column.at[begun]
            pltpu.make_async_copy(src, gathered.at[0, :, c // ZS, c % ZS], r_sem.at[0]).start()

    def around(k):
        for way in range(2):
            if k > 1:
                column_landed(k - 1, way)
            if k < 5:
                column_copy(k, way).start()
        if k == 1:
            place(0)
        elif k < 5:
            place(ZS - (k - 1))
            place(k - 1)
        else:
            place(4)

    if FIRST:
        around(1)
    for s in range(FIRST, NODES):

        @pl.when(shift != 0)
        def _():
            first_hop(s).start()

        @pl.when(shift == 0)
        def _():
            pltpu.make_async_copy(factor.at[s], middle.at[s], p_sem.at[s, 1]).start()

    def second_hop(s, way):
        where = same_lo if way == 0 else other_lo
        if s in SHARED:
            where = (x_hi * ZS + z, target)
        return remote(
            middle.at[s], gathered.at[s, :, c // ZS, c % ZS], q_sem.at[s, way], r_sem.at[s], where
        )

    def forward_piece(s):
        landed(middle.at[s], p_sem.at[s, 1])
        stays = c == target
        if s in SHARED:
            stays = jnp.logical_and(stays, x_hi == x_lo)
        else:
            second_hop(s, 1).start()

        @pl.when(jnp.logical_not(stays))
        def _():
            second_hop(s, 0).start()

        @pl.when(stays)
        def _():
            pltpu.make_async_copy(middle.at[s], gathered.at[s, :, c // ZS, c % ZS], r_sem.at[s]).start()

    across = (r, ((x_hi + 1) % 2) * (2 * YS) + y * 2 + core)

    def across_copy(s):
        return remote(
            factor.at[s], row_factor.at[s, x_hi, y, core], m_sem.at[s, 0], m_sem.at[s, 1], across
        )

    def cross_rows(s):
        across_copy(s).start()
        row_factor[s, x_hi, y, core] = factor[s]

    def row_copy(s, d):
        ref = row_factor.at[s, :, y, core]
        where = (r, x_hi * (2 * YS) + ((y + d) % YS) * 2 + core)
        return remote(ref, ref, m_sem.at[s, 2], m_sem.at[s, 3], where)

    def spread_rows(s):
        landed(row_factor.at[s, 1 - x_hi, y, core], m_sem.at[s, 1])
        for d in (2, 1, 3):
            row_copy(s, d).start()

    def rows_copy(s):
        ref = row_factor.at[s, :, :, core]
        return remote(ref, ref, m_sem.at[s, 4], m_sem.at[s, 5], mate)

    def share_rows(s):
        landed(row_factor.at[s, :, pl.ds(0, YS - 1), core], m_sem.at[s, 3])
        rows_copy(s).start()

    def ring_slice(s, q, shard):
        if s in SHARED:
            return gathered.at[s, q, x_lo, shard]
        return gathered.at[s, q, :, shard]

    def ring_copy(s, q, k, way):
        if way == 0:
            shard, where = slot_at((z + ZS - (k - 1)) % ZS), right
        else:
            shard, where = slot_at((z + (k - 1)) % ZS), left
        ref = ring_slice(s, q, shard)
        return remote(ref, ref, ring_send.at[s, q, way, k - 1], ring_recv.at[s, q, way, k - 1], where)

    def ring_landed(s, q, k, way):
        if way == 0:
            shard = slot_at((z + ZS - k) % ZS)
        else:
            shard = slot_at((z + k) % ZS)
        landed(ring_slice(s, q, shard), ring_recv.at[s, q, way, k - 1])

    def share_slice(s, at):
        ref = gathered.at[s, :, x_lo, slot_at(at % ZS)]
        remote(ref, ref, x_sem.at[0, s], x_sem.at[1, s], ((1 - x_lo) * ZS + z, c)).start()

    def ring(s, k):
        if k == 1:
            here = gathered.at[s, :, :, slot_at(z)]
            if s in SHARED:
                here = gathered.at[s, :, x_lo, slot_at(z)]
            landed(here, r_sem.at[s])
        for q in range(2):
            for way in range(2):
                if 1 < k < 5 or (k == 5 and way == q):
                    ring_landed(s, q, k - 1, way)
                if k < 4 or (k == 4 and way == q):
                    ring_copy(s, q, k, way).start()
        if s in SHARED:
            share_slice(s, z + k - 1)
            if 1 < k < 5:
                share_slice(s, z + ZS - (k - 1))

    def separate(s, m):
        if m == 0:
            loads[s].wait()

        def body(i, carry):
            at = pl.multiple_of(i * 64, 64)
            for q in range(2):
                dense[s, m, q, pl.ds(at, 64), :] = raw[s, m, pl.ds(at, 64), q, :]
            return carry

        lax.fori_loop(0, 8, body, 0)

    def core_copy(s, m):
        return remote(
            term.at[s, m, :, 1 - core], other.at[s, m], core_send.at[s, m], core_recv.at[s, m], mate
        )

    def products(s):
        if s < FIRST:
            landed(gathered.at[0], r_sem.at[0])
        if s in SHARED:
            landed(gathered.at[s, :, 1 - x_lo], x_sem.at[1, s])
        if s == 0:
            mask_load.wait()
        keep = [
            [-mask[s, m * ROWS + r, q * ROWS + c].astype(F32) for q in range(2)]
            for m in range(2)
        ]
        for m in range(2):
            def body(i, carry):
                at = pl.multiple_of(i * 256, 256)
                total = None
                for q in range(2):
                    right_side = gathered[s, q].reshape(512, 512)
                    part = keep[m][q] * jnp.dot(
                        dense[s, m, q, pl.ds(at, 256), :], right_side, preferred_element_type=F32
                    )
                    total = part if total is None else total + part
                term[s, m, pl.ds(i * 4, 4)] = total.reshape(4, 2, PIECE, 512)
                high = total.astype(BF16)
                split[m, 0, pl.ds(at, 256), :] = high
                split[m, 1, pl.ds(at, 256), :] = (total - high.astype(F32)).astype(BF16)
                return carry

            lax.fori_loop(0, 2, body, 0)
            core_copy(s, m).start()

    def t_copy(s, d):
        p = chip_peer(d)
        return remote(
            send_t.at[s, d - 1], recv_t.at[s, d - 1], t_sem.at[s, 0], t_sem.at[s, 1], (r, p * 2 + core)
        )

    def send_partials(s):
        for m in range(2):
            landed(other.at[s, m], core_recv.at[s, m])

        def join(p, top):
            for m in range(2):
                x = term[s, m, p, core] + other[s, m, p]
                term[s, m, p, core] = x
                top = jnp.maximum(top, jnp.abs(x))
            return top

        code = code_of(largest(lax.fori_loop(0, CHIPS, join, jnp.zeros((PIECE, 512), F32))))

        def body(d, carry):
            p = chip_peer(d)
            x = jnp.concatenate([term[s, m, p, core] for m in range(2)], axis=0)
            pack_into(send_t.at[s, d - 1], x, code)
            t_copy(s, d).start()
            return carry

        lax.fori_loop(1, CHIPS, body, 0)
        for m in range(2):
            cols[s, m] = term[s, m, chip, core]

    def cols_copy(s):
        return pltpu.make_async_copy(cols.at[s], cols_out.at[s], c_sem.at[s])

    def sum_columns(s):
        landed(recv_t.at[s], t_sem.at[s, 1])

        def body(d, carry):
            cols[s] += unpack(recv_t.at[s, d], 64).reshape(2, PIECE, 512)
            return carry

        lax.fori_loop(0, CHIPS - 1, body, 0)
        cols_copy(s).start()

    def half_copy(s):
        return remote(own_g.at[s, 1 - core], other_g.at[s], d_sem.at[s, 0], d_sem.at[s, 1], mate)

    def diagonal_terms(s):
        landed(row_factor.at[s, :, :, 1 - core], m_sem.at[s, 5])
        for half in (1 - core, core):
            total = None
            for m in range(2):
                at = pl.multiple_of(half * 256, 256)
                left_side = row_factor[s, :, :, :, m, :, pl.ds(at, 256)].reshape(512, 256)
                for part in range(2):
                    dot = lax.dot_general(
                        left_side, split[m, part], (((0,), (0,)), ((), ())), preferred_element_type=F32
                    )
                    total = dot if total is None else total + dot
            own_g[s, half] = total
            if half is not core:
                half_copy(s).start()

    def g_copy(s, d):
        return remote(
            send_g.at[s, d - 1], recv_g.at[s, d - 1], g_sem.at[s, 0], g_sem.at[s, 1], plane_device(d)
        )

    def send_terms(s):
        landed(other_g.at[s], d_sem.at[s, 1])
        whole = own_g[s, core] + other_g[s]
        own_g[s, core] = whole
        code = code_of(largest(whole))

        def body(d, carry):
            at = pl.multiple_of(plane_place(d) * 16, 16)
            pack_into(send_g.at[s, d - 1], own_g[s, core, pl.ds(at, 16), :], code)
            g_copy(s, d).start()
            return carry

        lax.fori_loop(1, PLANE, body, 0)

    def u_copy(s, d):
        ref = levels.at[s, z]
        return remote(ref, ref, u_sem.at[s, 0], u_sem.at[s, 1], (z_peer(d), c))

    def send_levels(s):
        landed(recv_g.at[s], g_sem.at[s, 1])
        mine = own_g[s, core, pl.ds(pl.multiple_of(place_here * 16, 16), 16), :]
        total = lax.fori_loop(0, PLANE - 1, lambda d, x: x + unpack(recv_g.at[s, d], 16), mine)
        pack_into(levels.at[s, z], total, code_of(largest(total)))

        def body(d, carry):
            u_copy(s, d).start()
            return carry

        lax.fori_loop(1, ZS, body, 0)

    def h_copy(s, d):
        ref = packed.at[s, core, place_here]
        return remote(ref, ref, h_sem.at[s, 0], h_sem.at[s, 1], plane_device(d))

    def send_diagonal(s):
        landed(levels.at[s, pl.ds(0, ZS - 1)], u_sem.at[s, 1])
        zero = jnp.zeros((16, 512), F32)
        total = lax.fori_loop(0, ZS, lambda i, x: x + unpack(levels.at[s, i], 16), zero)
        pack_into(packed.at[s, core, place_here], total, code_of(largest(total)))

        def body(d, carry):
            h_copy(s, d).start()
            return carry

        lax.fori_loop(1, PLANE, body, 0)

    def k_copy(s):
        ref = packed.at[s, core]
        return remote(ref, ref, k_sem.at[s, 0], k_sem.at[s, 1], mate)

    def share_diagonal(s):
        landed(recv_g.at[s], h_sem.at[s, 1])
        k_copy(s).start()

    def out_copy(s):
        return pltpu.make_async_copy(diag.at[s], diag_out.at[s], o_sem.at[s])

    def write_diagonal(s):
        landed(packed.at[s, 1 - core], k_sem.at[s, 1])

        def body(p, carry):
            for half in range(2):
                at = pl.multiple_of(half * 256 + p * 16, 16)
                diag[s, pl.ds(at, 16), :] = unpack(packed.at[s, half, p], 16)
            return carry

        lax.fori_loop(0, PLANE, body, 0)
        out_copy(s).start()

    stage = {
        "D": separate, "Z": around, "P": forward_piece, "B": cross_rows, "A": spread_rows, "F": share_rows, "R": ring,
        "1": products, "2": send_partials, "3": sum_columns, "4": diagonal_terms, "5": send_terms,
        "6": send_levels, "7": send_diagonal, "8": share_diagonal, "9": write_diagonal,
    }
    order = (
        "B0", "B1", "B2", "D00", "D01", "P0", "A0", "D10", "P1", "D11", "R01", "A1",
        "P2", "D20", "R02", "R11", "D21", "R03", "R12", "A2", "F0", "R04", "R13", "F1",
        "R05", "R14", "10", "R21", "40", "F2", "R15", "R22", "20", "50", "11", "R23",
        "R24", "21", "41", "51", "60", "R25", "12", "42", "52", "70", "61", "30",
        "62", "22", "80", "71", "72", "31", "81", "90", "82", "91", "32", "92",
    )
    for word in order:
        stage[word[0]](*(int(n) for n in word[1:]))

    if FIRST:
        for k in range(1, 5):
            for way in range(2):
                column_copy(k, way).wait_send()
        for i in range(ZS):
            place_copy(i, 1).wait_send()

            @pl.when(c != x_lo * ZS + (z + i) % ZS)
            def _():
                place_copy(i, 0).wait_send()

    for s in range(NODES):
        if s >= FIRST:

            @pl.when(shift != 0)
            def _():
                first_hop(s).wait_send()

            if s in SHARED:
                landed(gathered.at[s, :, x_lo], x_sem.at[0, s])

                @pl.when(jnp.logical_not(jnp.logical_and(c == target, x_hi == x_lo)))
                def _():
                    second_hop(s, 0).wait_send()

            else:

                @pl.when(c != target)
                def _():
                    second_hop(s, 0).wait_send()

                second_hop(s, 1).wait_send()

            for q in range(2):
                for k in range(1, 5):
                    for way in range(2):
                        if k < 4 or way == q:
                            ring_copy(s, q, k, way).wait_send()
        across_copy(s).wait_send()
        landed(row_factor.at[s, :, pl.ds(0, YS - 1), core], m_sem.at[s, 2])
        rows_copy(s).wait_send()
        for m in range(2):
            core_copy(s, m).wait_send()
        half_copy(s).wait_send()
        landed(send_t.at[s], t_sem.at[s, 0])
        landed(send_g.at[s], g_sem.at[s, 0])
        landed(levels.at[s, pl.ds(0, ZS - 1)], u_sem.at[s, 0])
        landed(recv_g.at[s], h_sem.at[s, 0])
        k_copy(s).wait_send()
        cols_copy(s).wait()
        out_copy(s).wait()


def shards(inverse_blocks, factor_cols, diag_inverse, block_mask):
    blocks = inverse_blocks.reshape(NODES, 2, 512, 2, 512)
    factor = factor_cols.reshape(NODES, 2, PIECE, 512)
    vmem = pltpu.VMEM
    dma = pltpu.SemaphoreType.DMA
    columns, term = pl.pallas_call(
        kernel,
        out_shape=(
            jax.ShapeDtypeStruct((NODES, 2, PIECE, 512), F32),
            jax.ShapeDtypeStruct((NODES, 512, 512), F32),
        ),
        in_specs=[
            pl.BlockSpec(memory_space=pltpu.HBM),
            pl.BlockSpec(memory_space=pltpu.HBM),
            pl.BlockSpec(memory_space=pltpu.HBM),
        ],
        out_specs=(
            pl.BlockSpec(memory_space=pl.ANY),
            pl.BlockSpec(memory_space=pl.ANY),
        ),
        scratch_shapes=[
            vmem((NODES, 2, 512, 2, 512), BF16),
            vmem((NODES, 2, 2, 512, 512), BF16),
            vmem((NODES, 2, PIECE, 512), BF16),
            vmem((NODES, 2, PIECE, 512), BF16),
            vmem((ZS, 2, PIECE, 512), BF16),
            vmem((NODES, 2, 2, ZS, PIECE, 512), BF16),
            vmem((NODES, 2, YS, 2, 2, PIECE, 512), BF16),
            vmem((NODES, 2, CHIPS, 2, PIECE, 512), F32),
            vmem((2, 2, 512, 512), BF16),
            vmem((NODES, 2, CHIPS, PIECE, 512), F32),
            vmem((NODES, CHIPS - 1, T_WORDS, 128), I32),
            vmem((NODES, CHIPS - 1, T_WORDS, 128), I32),
            vmem((NODES, 2, PIECE, 512), F32),
            vmem((NODES, 2, 256, 512), F32),
            vmem((NODES, 256, 512), F32),
            vmem((NODES, PLANE - 1, G_WORDS, 128), I32),
            vmem((NODES, PLANE - 1, G_WORDS, 128), I32),
            vmem((NODES, ZS, G_WORDS, 128), I32),
            vmem((NODES, 2, PLANE, G_WORDS, 128), I32),
            vmem((NODES, 512, 512), F32),
            pltpu.SMEM((NODES, 32, 32), I32),
            dma((NODES,)),
            dma((2,)),
            dma((NODES, 2)),
            dma((NODES, 2)),
            dma((NODES,)),
            dma((2, NODES)),
            dma((2, 2, 4)),
            dma((ZS, 2)),
            dma((NODES, 6)),
            dma((NODES, 2, 2, 4)),
            dma((NODES, 2, 2, 4)),
            dma((NODES, 2)),
            dma((NODES, 2)),
            dma((NODES, 2)),
            dma((NODES,)),
            dma((NODES, 2)),
            dma((NODES, 2)),
            dma((NODES, 2)),
            dma((NODES, 2)),
            dma((NODES, 2)),
            dma((NODES,)),
        ],
        compiler_params=pltpu.CompilerParams(
            collective_id=0, has_side_effects=True, vmem_limit_bytes=48 * 2**20
        ),
        cost_estimate=pl.CostEstimate(
            flops=NODES * 4 * 2 * 512**3, bytes_accessed=16 * 2**20, transcendentals=0
        ),
    )(blocks, factor, block_mask)
    inverse_cols = columns.reshape(NODES, 2, 1, PIECE, 512)
    return (inverse_cols, diag_inverse - term)


def solution(mesh):
    placed = (
        P(None, None, "prow", None, None, "pcol", None),
        P(None, None, "prow", "pcol", None),
        P(),
        P(),
    )
    return jax.shard_map(
        shards,
        mesh=mesh,
        in_specs=placed,
        out_specs=(P(None, None, "prow", "pcol", None), P()),
        check_vma=False,
    )
```

```python
import jax
import jax.numpy as jnp
from jax import lax
from jax.experimental import pallas as pl
from jax.experimental.pallas import tpu as pltpu
from jax.sharding import PartitionSpec as P

MESH = pl.DeviceIdType.MESH
F32 = jnp.float32
BF16 = jnp.bfloat16
I32 = jnp.int32

NODES = 3
ZS = 8
YS = 4
CHIPS = 8
ROWS = 16
PLANE = 16
FIRST = 0
SHARED = (1,)
PIECE = 32
T_WORDS = 136
G_WORDS = 40


def scale_of(code):
    value = code.astype(F32)
    return jnp.where(code > 0, value * (2.0**-8), value * (-(2.0**-30)))


def code_of(top):
    coarse = jnp.ceil(top * 256.0).astype(I32)
    fine = -jnp.maximum(jnp.ceil(jnp.minimum(top, 1.0) * (2.0**30)), 1.0).astype(I32)
    return jnp.where(top >= 1.0, coarse, fine)


def largest(x):
    return jnp.max(jnp.max(jnp.abs(x), axis=0, keepdims=True), axis=1, keepdims=True)


def pack_into(ref, x, code):
    rows = x.shape[0]
    inverse = 32767.0 / scale_of(code)
    q = jnp.floor(x * inverse + 0.5).astype(I32)
    for half in range(2):
        upper = q[:, half * 128 : half * 128 + 128]
        lower = q[:, 256 + half * 128 : 384 + half * 128]
        ref[half * rows : half * rows + rows, :] = (upper << 16) | (lower & 0xFFFF)
    ref[2 * rows : 2 * rows + 8, :] = jnp.broadcast_to(code, (8, 128))


def unpack(ref, rows):
    step = scale_of(ref[2 * rows : 2 * rows + 8, :])[0:1, :] * (1.0 / 32767.0)
    parts = []
    words = [ref[half * rows : half * rows + rows, :] for half in range(2)]
    for word in words:
        parts.append((word >> 16).astype(F32) * step)
    for word in words:
        parts.append(((word << 16) >> 16).astype(F32) * step)
    return jnp.concatenate(parts, axis=1)


def kernel(
    blocks, factor_in, mask_in, cols_out, diag_out,
    raw, dense, factor, middle, column, gathered, row_factor, term, split, other, send_t, recv_t, cols,
    own_g, other_g, send_g, recv_g, levels, packed, diag, mask,
    a_sem, l_sem, p_sem, q_sem, r_sem, x_sem, z_sem, y_sem, m_sem, ring_send, ring_recv, core_send, core_recv,
    t_sem, c_sem, d_sem, g_sem, u_sem, h_sem, k_sem, o_sem,
):
    r = lax.axis_index("prow")
    c = lax.axis_index("pcol")
    x_lo, z = r // ZS, r % ZS
    x_hi, y, core = c // (2 * YS), (c // 2) % YS, c % 2
    chip = c // 2
    mate = (r, chip * 2 + (1 - core))
    shift = y + YS * core
    origin = (z + ZS - shift) % ZS
    target = x_lo * ZS + origin

    def slot_at(where):
        gap = (where + ZS - c % ZS) % ZS
        return (gap % YS) * 2 + gap // YS

    def z_peer(d):
        j = d - 1
        step = 4 + j // 2 - (j % 2) * (2 * (j // 2) + 1)
        return x_lo * ZS + (z + step + ZS) % ZS

    place_here = (x_lo * 2 + x_hi) * YS + y

    def plane_peer(d):
        i, j = (d - 1) % 4, (d - 1) // 4
        step = 2 + j // 2 - (j % 2) * (2 * (j // 2) + 1)
        return (x_lo + (i + 1) // 2) % 2, (x_hi + 1 - i // 2) % 2, (y + step + YS) % YS

    def plane_device(d):
        lo, hi, at_y = plane_peer(d)
        return (lo * ZS + z, hi * (2 * YS) + at_y * 2 + core)

    def plane_place(d):
        lo, hi, at_y = plane_peer(d)
        return (lo * 2 + hi) * YS + at_y

    def chip_peer(d):
        j = (d - 1) // 2
        step = 2 + j // 2 - (j % 2) * (2 * (j // 2) + 1)
        return ((x_hi + d % 2) % 2) * YS + (y + step + YS) % YS

    def remote(src, dst, send, recv, where):
        return pltpu.make_async_remote_copy(
            src_ref=src, dst_ref=dst, send_sem=send, recv_sem=recv, device_id=where, device_id_type=MESH
        )

    def landed(ref, sem):
        pltpu.make_async_copy(ref, ref, sem).wait()

    own_load = pltpu.make_async_copy(factor_in, factor, l_sem.at[0])
    own_load.start()
    mask_load = pltpu.make_async_copy(mask_in, mask, l_sem.at[1])
    mask_load.start()
    loads = [
        pltpu.make_async_copy(blocks.at[s], raw.at[s], a_sem.at[s]) for s in range(NODES)
    ]
    for load in loads:
        load.start()

    barrier = pltpu.get_barrier_semaphore()

    def greet(where):
        pl.semaphore_signal(barrier, inc=1, device_id=where, device_id_type=MESH)

    same_lo = (r, target)
    other_lo = ((r + ZS) % ROWS, target)
    has_self = c == target if FIRST == 0 else c // ZS == x_lo
    rounds = 1 if FIRST == 0 else ZS

    def greet_plane(i, carry):
        for lo in range(2):
            if FIRST == 0:
                there = (lo * ZS + z, target)
                back = ((c // ZS) * ZS + z, lo * ZS + slot_at(z))
            else:
                there = (lo * ZS + z, x_lo * ZS + i)
                back = ((c // ZS) * ZS + z, lo * ZS + i)

            @pl.when(jnp.logical_not(jnp.logical_and(there[0] == r, there[1] == c)))
            def _():
                greet(there)

            @pl.when(jnp.logical_not(jnp.logical_and(back[0] == r, back[1] == c)))
            def _():
                greet(back)

        return carry

    lax.fori_loop(0, rounds, greet_plane, 0)
    greet(mate)

    def greet_z(d, carry):
        greet((z_peer(d), c))
        return carry

    lax.fori_loop(1, ZS, greet_z, 0)

    def greet_xy(d, carry):
        greet(plane_device(d))
        return carry

    lax.fori_loop(1, PLANE, greet_xy, 0)
    own_load.wait()

    partners = 4 * rounds + 1 + (ZS - 1) + (PLANE - 1)

    @pl.when(jnp.logical_not(has_self))
    def _():
        pl.semaphore_wait(barrier, partners)

    @pl.when(has_self)
    def _():
        pl.semaphore_wait(barrier, partners - 2)

    def first_hop(s):
        where = (x_lo * ZS + (z + shift) % ZS, c)
        return remote(factor.at[s], middle.at[s], p_sem.at[s, 0], p_sem.at[s, 1], where)

    right = (x_lo * ZS + (z + 1) % ZS, c)
    left = (x_lo * ZS + (z + ZS - 1) % ZS, c)

    def column_copy(k, way):
        if way == 0:
            begun, where = (z + ZS - (k - 1)) % ZS, right
        else:
            begun, where = (z + (k - 1)) % ZS, left
        ref = column.at[begun] if k < 4 else column.at[begun, way]
        src = ref if k > 1 else factor.at[0]
        return remote(src, ref, z_sem.at[0, way, k - 1], z_sem.at[1, way, k - 1], where)

    def column_landed(k, way):
        begun = (z + ZS - k) % ZS if way == 0 else (z + k) % ZS
        landed(column.at[begun] if k < 4 else column.at[begun, way], z_sem.at[1, way, k - 1])

    def place_copy(i, lo):
        begun = (z + i) % ZS
        src = factor.at[0] if i == 0 else column.at[begun]
        where = (((x_lo + lo) % 2) * ZS + z, x_lo * ZS + begun)
        return remote(src, gathered.at[0, :, c // ZS, c % ZS], y_sem.at[i, lo], r_sem.at[0], where)

    def place(i):
        begun = (z + i) % ZS
        place_copy(i, 1).start()

        @pl.when(c != x_lo * ZS + begun)
        def _():
            place_copy(i, 0).start()

        @pl.when(c == x_lo * ZS + begun)
        def _():
            src = factor.at[0] if i == 0 else column.at[begun]
            pltpu.make_async_copy(src, gathered.at[0, :, c // ZS, c % ZS], r_sem.at[0]).start()

    def around(k):
        for way in range(2):
            if k > 1:
                column_landed(k - 1, way)
            if k < 5:
                column_copy(k, way).start()
        if k == 1:
            place(0)
        elif k < 5:
            place(ZS - (k - 1))
            place(k - 1)
        else:
            place(4)

    if FIRST:
        around(1)
    for s in range(FIRST, NODES):

        @pl.when(shift != 0)
        def _():
            first_hop(s).start()

        @pl.when(shift == 0)
        def _():
            pltpu.make_async_copy(factor.at[s], middle.at[s], p_sem.at[s, 1]).start()

    def second_hop(s, way):
        where = same_lo if way == 0 else other_lo
        if s in SHARED:
            where = (x_hi * ZS + z, target)
        return remote(
            middle.at[s], gathered.at[s, :, c // ZS, c % ZS], q_sem.at[s, way], r_sem.at[s], where
        )

    def forward_piece(s):
        landed(middle.at[s], p_sem.at[s, 1])
        stays = c == target
        if s in SHARED:
            stays = jnp.logical_and(stays, x_hi == x_lo)
        else:
            second_hop(s, 1).start()

        @pl.when(jnp.logical_not(stays))
        def _():
            second_hop(s, 0).start()

        @pl.when(stays)
        def _():
            pltpu.make_async_copy(middle.at[s], gathered.at[s, :, c // ZS, c % ZS], r_sem.at[s]).start()

    across = (r, ((x_hi + 1) % 2) * (2 * YS) + y * 2 + core)

    def across_copy(s):
        return remote(
            factor.at[s], row_factor.at[s, x_hi, y, core], m_sem.at[s, 0], m_sem.at[s, 1], across
        )

    def cross_rows(s):
        across_copy(s).start()
        row_factor[s, x_hi, y, core] = factor[s]

    def row_copy(s, d):
        ref = row_factor.at[s, :, y, core]
        where = (r, x_hi * (2 * YS) + ((y + d) % YS) * 2 + core)
        return remote(ref, ref, m_sem.at[s, 2], m_sem.at[s, 3], where)

    def spread_rows(s):
        landed(row_factor.at[s, 1 - x_hi, y, core], m_sem.at[s, 1])
        for d in (2, 1, 3):
            row_copy(s, d).start()

    def rows_copy(s):
        ref = row_factor.at[s, :, :, core]
        return remote(ref, ref, m_sem.at[s, 4], m_sem.at[s, 5], mate)

    def share_rows(s):
        landed(row_factor.at[s, :, pl.ds(0, YS - 1), core], m_sem.at[s, 3])
        rows_copy(s).start()

    def ring_slice(s, q, shard):
        if s in SHARED:
            return gathered.at[s, q, x_lo, shard]
        return gathered.at[s, q, :, shard]

    def ring_copy(s, q, k, way):
        if way == 0:
            shard, where = slot_at((z + ZS - (k - 1)) % ZS), right
        else:
            shard, where = slot_at((z + (k - 1)) % ZS), left
        ref = ring_slice(s, q, shard)
        return remote(ref, ref, ring_send.at[s, q, way, k - 1], ring_recv.at[s, q, way, k - 1], where)

    def ring_landed(s, q, k, way):
        if way == 0:
            shard = slot_at((z + ZS - k) % ZS)
        else:
            shard = slot_at((z + k) % ZS)
        landed(ring_slice(s, q, shard), ring_recv.at[s, q, way, k - 1])

    def share_slice(s, at):
        ref = gathered.at[s, :, x_lo, slot_at(at % ZS)]
        remote(ref, ref, x_sem.at[0, s], x_sem.at[1, s], ((1 - x_lo) * ZS + z, c)).start()

    def ring(s, k):
        if k == 1:
            here = gathered.at[s, :, :, slot_at(z)]
            if s in SHARED:
                here = gathered.at[s, :, x_lo, slot_at(z)]
            landed(here, r_sem.at[s])
        for q in range(2):
            for way in range(2):
                if 1 < k < 5 or (k == 5 and way == q):
                    ring_landed(s, q, k - 1, way)
                if k < 4 or (k == 4 and way == q):
                    ring_copy(s, q, k, way).start()
        if s in SHARED:
            share_slice(s, z + k - 1)
            if 1 < k < 5:
                share_slice(s, z + ZS - (k - 1))

    def separate(s, m):
        if m == 0:
            loads[s].wait()

        def body(i, carry):
            at = pl.multiple_of(i * 64, 64)
            for q in range(2):
                dense[s, m, q, pl.ds(at, 64), :] = raw[s, m, pl.ds(at, 64), q, :]
            return carry

        lax.fori_loop(0, 8, body, 0)

    def core_copy(s, m):
        return remote(
            term.at[s, m, :, 1 - core], other.at[s, m], core_send.at[s, m], core_recv.at[s, m], mate
        )

    def products(s):
        if s < FIRST:
            landed(gathered.at[0], r_sem.at[0])
        if s in SHARED:
            landed(gathered.at[s, :, 1 - x_lo], x_sem.at[1, s])
        if s == 0:
            mask_load.wait()
        keep = [
            [-mask[s, m * ROWS + r, q * ROWS + c].astype(F32) for q in range(2)]
            for m in range(2)
        ]
        for m in range(2):
            def body(i, carry):
                at = pl.multiple_of(i * 256, 256)
                total = None
                for q in range(2):
                    right_side = gathered[s, q].reshape(512, 512)
                    part = keep[m][q] * jnp.dot(
                        dense[s, m, q, pl.ds(at, 256), :], right_side, preferred_element_type=F32
                    )
                    total = part if total is None else total + part
                term[s, m, pl.ds(i * 4, 4)] = total.reshape(4, 2, PIECE, 512)
                high = total.astype(BF16)
                split[m, 0, pl.ds(at, 256), :] = high
                split[m, 1, pl.ds(at, 256), :] = (total - high.astype(F32)).astype(BF16)
                return carry

            lax.fori_loop(0, 2, body, 0)
            core_copy(s, m).start()

    def t_copy(s, d):
        p = chip_peer(d)
        return remote(
            send_t.at[s, d - 1], recv_t.at[s, d - 1], t_sem.at[s, 0], t_sem.at[s, 1], (r, p * 2 + core)
        )

    def send_partials(s):
        for m in range(2):
            landed(other.at[s, m], core_recv.at[s, m])

        def join(p, top):
            for m in range(2):
                x = term[s, m, p, core] + other[s, m, p]
                term[s, m, p, core] = x
                top = jnp.maximum(top, jnp.abs(x))
            return top

        code = code_of(largest(lax.fori_loop(0, CHIPS, join, jnp.zeros((PIECE, 512), F32))))

        def body(d, carry):
            p = chip_peer(d)
            x = jnp.concatenate([term[s, m, p, core] for m in range(2)], axis=0)
            pack_into(send_t.at[s, d - 1], x, code)
            t_copy(s, d).start()
            return carry

        lax.fori_loop(1, CHIPS, body, 0)
        for m in range(2):
            cols[s, m] = term[s, m, chip, core]

    def cols_copy(s):
        return pltpu.make_async_copy(cols.at[s], cols_out.at[s], c_sem.at[s])

    def sum_columns(s):
        landed(recv_t.at[s], t_sem.at[s, 1])

        def body(d, carry):
            cols[s] += unpack(recv_t.at[s, d], 64).reshape(2, PIECE, 512)
            return carry

        lax.fori_loop(0, CHIPS - 1, body, 0)
        cols_copy(s).start()

    def half_copy(s):
        return remote(own_g.at[s, 1 - core], other_g.at[s], d_sem.at[s, 0], d_sem.at[s, 1], mate)

    def diagonal_terms(s):
        landed(row_factor.at[s, :, :, 1 - core], m_sem.at[s, 5])
        for half in (1 - core, core):
            total = None
            for m in range(2):
                at = pl.multiple_of(half * 256, 256)
                left_side = row_factor[s, :, :, :, m, :, pl.ds(at, 256)].reshape(512, 256)
                for part in range(2):
                    dot = lax.dot_general(
                        left_side, split[m, part], (((0,), (0,)), ((), ())), preferred_element_type=F32
                    )
                    total = dot if total is None else total + dot
            own_g[s, half] = total
            if half is not core:
                half_copy(s).start()

    def g_copy(s, d):
        return remote(
            send_g.at[s, d - 1], recv_g.at[s, d - 1], g_sem.at[s, 0], g_sem.at[s, 1], plane_device(d)
        )

    def send_terms(s):
        landed(other_g.at[s], d_sem.at[s, 1])
        whole = own_g[s, core] + other_g[s]
        own_g[s, core] = whole
        code = code_of(largest(whole))

        def body(d, carry):
            at = pl.multiple_of(plane_place(d) * 16, 16)
            pack_into(send_g.at[s, d - 1], own_g[s, core, pl.ds(at, 16), :], code)
            g_copy(s, d).start()
            return carry

        lax.fori_loop(1, PLANE, body, 0)

    def u_copy(s, d):
        ref = levels.at[s, z]
        return remote(ref, ref, u_sem.at[s, 0], u_sem.at[s, 1], (z_peer(d), c))

    def send_levels(s):
        landed(recv_g.at[s], g_sem.at[s, 1])
        mine = own_g[s, core, pl.ds(pl.multiple_of(place_here * 16, 16), 16), :]
        total = lax.fori_loop(0, PLANE - 1, lambda d, x: x + unpack(recv_g.at[s, d], 16), mine)
        pack_into(levels.at[s, z], total, code_of(largest(total)))

        def body(d, carry):
            u_copy(s, d).start()
            return carry

        lax.fori_loop(1, ZS, body, 0)

    def h_copy(s, d):
        ref = packed.at[s, core, place_here]
        return remote(ref, ref, h_sem.at[s, 0], h_sem.at[s, 1], plane_device(d))

    def send_diagonal(s):
        landed(levels.at[s, pl.ds(0, ZS - 1)], u_sem.at[s, 1])
        zero = jnp.zeros((16, 512), F32)
        total = lax.fori_loop(0, ZS, lambda i, x: x + unpack(levels.at[s, i], 16), zero)
        pack_into(packed.at[s, core, place_here], total, code_of(largest(total)))

        def body(d, carry):
            h_copy(s, d).start()
            return carry

        lax.fori_loop(1, PLANE, body, 0)

    def k_copy(s):
        ref = packed.at[s, core]
        return remote(ref, ref, k_sem.at[s, 0], k_sem.at[s, 1], mate)

    def share_diagonal(s):
        landed(recv_g.at[s], h_sem.at[s, 1])
        k_copy(s).start()

    def out_copy(s):
        return pltpu.make_async_copy(diag.at[s], diag_out.at[s], o_sem.at[s])

    def write_diagonal(s):
        landed(packed.at[s, 1 - core], k_sem.at[s, 1])

        def body(p, carry):
            for half in range(2):
                at = pl.multiple_of(half * 256 + p * 16, 16)
                diag[s, pl.ds(at, 16), :] = unpack(packed.at[s, half, p], 16)
            return carry

        lax.fori_loop(0, PLANE, body, 0)
        out_copy(s).start()

    stage = {
        "D": separate, "Z": around, "P": forward_piece, "B": cross_rows, "A": spread_rows, "F": share_rows, "R": ring,
        "1": products, "2": send_partials, "3": sum_columns, "4": diagonal_terms, "5": send_terms,
        "6": send_levels, "7": send_diagonal, "8": share_diagonal, "9": write_diagonal,
    }
    order = (
        "B0", "B1", "B2", "D00", "D01", "P0", "A0", "D10", "P1", "D11", "R01", "A1",
        "P2", "D20", "R02", "R11", "D21", "R03", "R12", "A2", "F0", "R04", "R13", "F1",
        "R21", "R05", "R14", "10", "R22", "40", "F2", "R15", "R23", "20", "50", "11",
        "R24", "21", "41", "51", "60", "R25", "12", "42", "52", "70", "61", "30",
        "62", "22", "80", "71", "72", "31", "81", "90", "82", "91", "32", "92",
    )
    for word in order:
        stage[word[0]](*(int(n) for n in word[1:]))

    if FIRST:
        for k in range(1, 5):
            for way in range(2):
                column_copy(k, way).wait_send()
        for i in range(ZS):
            place_copy(i, 1).wait_send()

            @pl.when(c != x_lo * ZS + (z + i) % ZS)
            def _():
                place_copy(i, 0).wait_send()

    for s in range(NODES):
        if s >= FIRST:

            @pl.when(shift != 0)
            def _():
                first_hop(s).wait_send()

            if s in SHARED:
                landed(gathered.at[s, :, x_lo], x_sem.at[0, s])

                @pl.when(jnp.logical_not(jnp.logical_and(c == target, x_hi == x_lo)))
                def _():
                    second_hop(s, 0).wait_send()

            else:

                @pl.when(c != target)
                def _():
                    second_hop(s, 0).wait_send()

                second_hop(s, 1).wait_send()

            for q in range(2):
                for k in range(1, 5):
                    for way in range(2):
                        if k < 4 or way == q:
                            ring_copy(s, q, k, way).wait_send()
        across_copy(s).wait_send()
        landed(row_factor.at[s, :, pl.ds(0, YS - 1), core], m_sem.at[s, 2])
        rows_copy(s).wait_send()
        for m in range(2):
            core_copy(s, m).wait_send()
        half_copy(s).wait_send()
        landed(send_t.at[s], t_sem.at[s, 0])
        landed(send_g.at[s], g_sem.at[s, 0])
        landed(levels.at[s, pl.ds(0, ZS - 1)], u_sem.at[s, 0])
        landed(recv_g.at[s], h_sem.at[s, 0])
        k_copy(s).wait_send()
        cols_copy(s).wait()
        out_copy(s).wait()


def shards(inverse_blocks, factor_cols, diag_inverse, block_mask):
    blocks = inverse_blocks.reshape(NODES, 2, 512, 2, 512)
    factor = factor_cols.reshape(NODES, 2, PIECE, 512)
    vmem = pltpu.VMEM
    dma = pltpu.SemaphoreType.DMA
    columns, term = pl.pallas_call(
        kernel,
        out_shape=(
            jax.ShapeDtypeStruct((NODES, 2, PIECE, 512), F32),
            jax.ShapeDtypeStruct((NODES, 512, 512), F32),
        ),
        in_specs=[
            pl.BlockSpec(memory_space=pltpu.HBM),
            pl.BlockSpec(memory_space=pltpu.HBM),
            pl.BlockSpec(memory_space=pltpu.HBM),
        ],
        out_specs=(
            pl.BlockSpec(memory_space=pl.ANY),
            pl.BlockSpec(memory_space=pl.ANY),
        ),
        scratch_shapes=[
            vmem((NODES, 2, 512, 2, 512), BF16),
            vmem((NODES, 2, 2, 512, 512), BF16),
            vmem((NODES, 2, PIECE, 512), BF16),
            vmem((NODES, 2, PIECE, 512), BF16),
            vmem((ZS, 2, PIECE, 512), BF16),
            vmem((NODES, 2, 2, ZS, PIECE, 512), BF16),
            vmem((NODES, 2, YS, 2, 2, PIECE, 512), BF16),
            vmem((NODES, 2, CHIPS, 2, PIECE, 512), F32),
            vmem((2, 2, 512, 512), BF16),
            vmem((NODES, 2, CHIPS, PIECE, 512), F32),
            vmem((NODES, CHIPS - 1, T_WORDS, 128), I32),
            vmem((NODES, CHIPS - 1, T_WORDS, 128), I32),
            vmem((NODES, 2, PIECE, 512), F32),
            vmem((NODES, 2, 256, 512), F32),
            vmem((NODES, 256, 512), F32),
            vmem((NODES, PLANE - 1, G_WORDS, 128), I32),
            vmem((NODES, PLANE - 1, G_WORDS, 128), I32),
            vmem((NODES, ZS, G_WORDS, 128), I32),
            vmem((NODES, 2, PLANE, G_WORDS, 128), I32),
            vmem((NODES, 512, 512), F32),
            pltpu.SMEM((NODES, 32, 32), I32),
            dma((NODES,)),
            dma((2,)),
            dma((NODES, 2)),
            dma((NODES, 2)),
            dma((NODES,)),
            dma((2, NODES)),
            dma((2, 2, 4)),
            dma((ZS, 2)),
            dma((NODES, 6)),
            dma((NODES, 2, 2, 4)),
            dma((NODES, 2, 2, 4)),
            dma((NODES, 2)),
            dma((NODES, 2)),
            dma((NODES, 2)),
            dma((NODES,)),
            dma((NODES, 2)),
            dma((NODES, 2)),
            dma((NODES, 2)),
            dma((NODES, 2)),
            dma((NODES, 2)),
            dma((NODES,)),
        ],
        compiler_params=pltpu.CompilerParams(
            collective_id=0, has_side_effects=True, vmem_limit_bytes=48 * 2**20
        ),
        cost_estimate=pl.CostEstimate(
            flops=NODES * 4 * 2 * 512**3, bytes_accessed=16 * 2**20, transcendentals=0
        ),
    )(blocks, factor, block_mask)
    inverse_cols = columns.reshape(NODES, 2, 1, PIECE, 512)
    return (inverse_cols, diag_inverse - term)


def solution(mesh):
    placed = (
        P(None, None, "prow", None, None, "pcol", None),
        P(None, None, "prow", "pcol", None),
        P(),
        P(),
    )
    return jax.shard_map(
        shards,
        mesh=mesh,
        in_specs=placed,
        out_specs=(P(None, None, "prow", "pcol", None), P()),
        check_vma=False,
    )
```
